32 devices in a mesh: win: 1, doc: 32 (over z, y, x, core), layer: 1.
Axes of the slice: x: 2, y: 2, z: 4, core: 2. Of those that a mesh axis runs over, the one named last changes fastest.
Arguments:
- pool_grads: bfloat16 [2, 16384, 4096], P('layer', ('win', 'doc')), may hold values from -6 to 6
- doc_ids: int32 [32, 512], P(('win', 'doc')), may hold values from 0 to 511, each once within a row
- query_grads: bfloat16 [2, 4096, 512], P('layer', 'doc'), may hold values from -6 to 6
- u_out: float32 [2, 64, 64], P('layer'), may hold values from -0.75 to 0.75
- u_in: float32 [2, 64, 64], P('layer'), may hold values from -0.75 to 0.75
- eigval: float32 [2, 64, 64], P('layer'), may hold values from 0.05 to 5
Outputs:
- scores: float32 [512, 16384], P('layer', ('win', 'doc'))
The draws below stay inside these ranges and needn't reach their ends.
Inputs may be any that keep to these rules, and one draw needn't show every extreme that they name: Each row of doc_ids is a permutation of 0 to 511.
All inputs are finite; a program needn't handle non-finite values.
Results may differ from the reference program's by a relative error of at most 0.0029.
Values may be sent and summed in bfloat16 or wider, within the bound.
A program may use at most 128 MiB of HBM per device.

```python
import math
import jax
import jax.numpy as jnp
from jax import lax

D_OUT = 64
D_IN = 64
QUERIES = 512
DOC_DEV = 512
LAYERS = 2
DOCS = 16384
BLOCKS = 32


def steps_of(own_key, dims, cuts, low, top_value):
    factor_of = 1.0
    for axis_at, parts in cuts:
        heights = jax.random.uniform(jax.random.fold_in(jax.random.fold_in(own_key, 6), axis_at), (parts,), jnp.float32, low / len(cuts), top_value / len(cuts))
        factor_of = factor_of * jnp.repeat(jnp.exp(heights), dims[axis_at] // parts).reshape((-1,) + (1,) * (len(dims) - 1 - axis_at))
    return factor_of


def noise(rng, dims, width, most, cuts=(), kind=jnp.bfloat16):
    factor_of = steps_of(rng, dims, cuts, -0.22, 0.18) if cuts else 1.0
    result = jax.random.normal(rng, dims, jnp.float32) * width * factor_of
    return jnp.minimum(jnp.maximum(result, -most), most).astype(kind)


def setup_inputs(seed: int = 0, part: int = 0) -> dict:
    arg_keys = jax.random.split(jax.random.key(seed), 7)
    part_splits = jax.random.split(jax.random.fold_in(arg_keys[6], part), 7)
    pool_grads = noise(part_splits[0], (LAYERS, DOCS, D_OUT * D_IN), 1.0, 6.0, ((1, 32),))
    doc_ids = jax.vmap(lambda own: jax.random.permutation(own, DOC_DEV))(jax.random.split(part_splits[1], BLOCKS)).reshape((BLOCKS, DOC_DEV)).astype(jnp.int32)
    query_grads = noise(arg_keys[2], (LAYERS, D_OUT * D_IN, QUERIES), 1.0, 6.0, ((1, 32),))
    u_out = noise(arg_keys[3], (LAYERS, D_OUT, D_OUT), D_OUT ** -0.5, 0.75, (), jnp.float32)
    u_in = noise(arg_keys[4], (LAYERS, D_IN, D_IN), D_IN ** -0.5, 0.75, (), jnp.float32)
    eigval = jnp.clip(jnp.exp(jax.random.uniform(arg_keys[5], (LAYERS, D_OUT, D_IN), jnp.float32, math.log(0.05), math.log(5.0))), 0.05, 5.0)
    return {"pool_grads": pool_grads, "doc_ids": doc_ids, "query_grads": query_grads, "u_out": u_out, "u_in": u_in, "eigval": eigval}


HIGH = lax.Precision.HIGHEST
DAMPING = 0.05

def precondition(raw, u_out, u_in, eigval):
    grid = raw.astype(jnp.float32).reshape(D_OUT, D_IN, -1)
    rotated = jnp.einsum('ac,abq->cbq', u_out, grid, precision=HIGH)
    rotated = jnp.einsum('bd,cbq->cdq', u_in, rotated, precision=HIGH)
    scaled = rotated / (eigval[:, :, None] + DAMPING)
    back = jnp.einsum('ac,cdq->adq', u_out, scaled, precision=HIGH)
    back = jnp.einsum('bd,adq->abq', u_in, back, precision=HIGH)
    return back.reshape(D_OUT * D_IN, -1).astype(jnp.bfloat16)

def reference(pool_grads, doc_ids, query_grads, u_out, u_in, eigval):
    offsets = jnp.arange(BLOCKS, dtype=jnp.int32)[:, None] * DOC_DEV
    rows = (offsets + doc_ids).reshape(-1).astype(jnp.int32)
    docs = jnp.take(pool_grads, rows, axis=1)

    def one_layer(total, pieces):
        raw, doc_rows, left, right, values = pieces
        prepared = precondition(raw, left, right, values)
        term = lax.dot_general(prepared, doc_rows, (((0,), (1,)), ((), ())), preferred_element_type=jnp.float32)
        return (total + term, None)
    start = jnp.zeros((QUERIES, DOC_DEV * BLOCKS), jnp.float32)
    total, _ = lax.scan(one_layer, start, (query_grads, docs, u_out, u_in, eigval))
    return total * (1.0 / math.sqrt(D_OUT * D_IN))
```

```python
import functools
import math

import jax
import jax.numpy as jnp
from jax import lax
from jax.experimental import pallas as pl
from jax.experimental.pallas import tpu as pltpu
from jax.sharding import PartitionSpec as P

D_OUT = 64
D_IN = 64

HIGH = lax.Precision.HIGHEST
DAMPING = 0.05
MESH = pl.DeviceIdType.MESH


def gather_kernel(nz, own_ref, out, rz, rx, ry, rxh, ryh, rc, su, sd, sx, sy, sxh, syh, sc, local):
    me = lax.axis_index("doc")
    rows, cols = own_ref.shape
    half = cols // 2
    z = me // 8
    low = lax.rem(me, 8)
    core = lax.rem(low, 2)
    x = lax.rem(low // 2, 2)
    y = low // 4
    base = low - core
    col_x = base + 2 - 4 * x
    col_y = base + 4 - 8 * y
    col_xy = base + 6 - 4 * x - 8 * y
    z0 = z * 8
    to_x = z0 + col_x + core
    to_y = z0 + col_y + core
    to_c = z0 + base + 1 - core

    barrier = pltpu.get_barrier_semaphore()
    for who in (to_x, to_y, to_c):
        pl.semaphore_signal(barrier, inc=1, device_id={"doc": who}, device_id_type=MESH)

    @pl.when(z < nz - 1)
    def _():
        pl.semaphore_signal(barrier, inc=1, device_id={"doc": me + 8}, device_id_type=MESH)

    @pl.when(z > 0)
    def _():
        pl.semaphore_signal(barrier, inc=1, device_id={"doc": me - 8}, device_id_type=MESH)

    pl.semaphore_wait(barrier, 3 + jnp.minimum(z, 1) + jnp.minimum(nz - 1 - z, 1))

    def block(column, zs, c, part=None):
        row = pl.multiple_of((zs * 8 + column + c) * rows, rows)
        if part is None:
            return out.at[pl.ds(row, rows), :]
        return out.at[pl.ds(row, rows), pl.ds(part * half, half)]

    def copy(ref, dst, send, recv, who):
        return pltpu.make_async_remote_copy(
            src_ref=ref, dst_ref=dst, send_sem=send, recv_sem=recv,
            device_id={"doc": who}, device_id_type=MESH,
        )

    def up(zs, ref):
        return copy(ref, block(base, zs, core), su.at[zs], rz.at[zs], me + 8)

    def down(zs, ref):
        return copy(ref, block(base, zs, core), sd.at[zs], rz.at[zs], me - 8)

    def along_x(zs, ref):
        return copy(ref, block(base, zs, core), sx.at[zs], rx.at[zs], to_x)

    def along_y(zs, ref):
        return copy(ref, block(base, zs, core), sy.at[zs], ry.at[zs], to_y)

    def half_x(zs):
        b = block(col_y, zs, core, 1)
        return copy(b, b, sxh.at[zs], rxh.at[zs], to_x)

    def half_y(zs):
        b = block(col_x, zs, core, 0)
        return copy(b, b, syh.at[zs], ryh.at[zs], to_y)

    def other(kind, zs, ref, b):
        at = zs + kind * nz
        return copy(ref, b, sc.at[at], rc.at[at], to_c)

    own_block = block(base, z, core)
    keep = pltpu.make_async_copy(own_ref, own_block, local)

    def column_out(zs, ref):
        along_x(zs, ref).start()
        along_y(zs, ref).start()
        other(0, zs, ref, block(base, zs, core)).start()

    def steps(k, act):
        if k == 0:
            act(z, 0)
            return

        @pl.when(z - k >= 0)
        def _():
            act(z - k, 1)

        @pl.when(z + k < nz)
        def _():
            act(z + k, -1)

    def from_column(zs, way):
        b = block(base, zs, core)
        if way == 1:
            copy(b, b, su.at[zs], rz.at[zs], me - 8).wait_recv()

            @pl.when(z < nz - 1)
            def _():
                up(zs, b).start()
        else:
            copy(b, b, sd.at[zs], rz.at[zs], me + 8).wait_recv()

            @pl.when(z > 0)
            def _():
                down(zs, b).start()
        column_out(zs, b)

    def from_sides(zs, way):
        b = block(col_x, zs, core)
        copy(b, b, sx.at[zs], rx.at[zs], to_x).wait_recv()
        half_y(zs).start()
        other(1, zs, b, b).start()
        b = block(col_y, zs, core)
        copy(b, b, sy.at[zs], ry.at[zs], to_y).wait_recv()
        half_x(zs).start()
        other(2, zs, b, b).start()

    def from_corner(zs, way):
        b = block(col_xy, zs, core, 1)
        copy(b, b, sxh.at[zs], rxh.at[zs], to_x).wait_recv()
        other(3, zs, b, b).start()
        b = block(col_xy, zs, core, 0)
        copy(b, b, syh.at[zs], ryh.at[zs], to_y).wait_recv()
        other(4, zs, b, b).start()

    @pl.when(z < nz - 1)
    def _():
        up(z, own_ref).start()

    @pl.when(z > 0)
    def _():
        down(z, own_ref).start()

    column_out(z, own_ref)
    keep.start()
    for k in range(1, nz):
        steps(k, from_column)
        steps(k - 1, from_sides)
    steps(nz - 1, from_sides)
    for k in range(nz):
        steps(k, from_corner)

    keep.wait()
    for zs in range(nz):
        b = block(base, zs, core)
        along_x(zs, b).wait_send()
        along_y(zs, b).wait_send()
        half_x(zs).wait_send()
        half_y(zs).wait_send()

        @pl.when((z < nz - 1) & (zs <= z))
        def _():
            up(zs, b).wait_send()

        @pl.when((z > 0) & (zs >= z))
        def _():
            down(zs, b).wait_send()

        for kind, column, part in ((0, base, None), (1, col_x, None), (2, col_y, None), (3, col_xy, 1), (4, col_xy, 0)):
            b = block(column, zs, core, part)
            other(kind, zs, b, b).wait_send()
            b = block(column, zs, 1 - core, part)
            other(kind, zs, b, b).wait_recv()


def gather_chips(own, doc):
    nz = doc // 8
    rows, cols = own.shape
    dma = pltpu.SemaphoreType.DMA
    return pl.pallas_call(
        functools.partial(gather_kernel, nz),
        out_shape=jax.ShapeDtypeStruct((rows * doc, cols), own.dtype),
        in_specs=[pl.BlockSpec(memory_space=pl.ANY)],
        out_specs=pl.BlockSpec(memory_space=pl.ANY),
        scratch_shapes=[dma((nz,))] * 5 + [dma((5 * nz,))] + [dma((nz,))] * 6 + [dma((5 * nz,)), dma],
        compiler_params=pltpu.CompilerParams(collective_id=0, has_side_effects=True),
    )(own)


def precondition(raw, u_out, u_in, eigval):
    rotated = jnp.einsum("lac,qlab->lqcb", u_out, raw, precision=HIGH)
    rotated = jnp.einsum("lbd,lqcb->lqcd", u_in, rotated, precision=HIGH)
    scaled = rotated / (eigval[:, None] + DAMPING)
    back = jnp.einsum("lac,lqcd->lqad", u_out, scaled, precision=HIGH)
    back = jnp.einsum("lbd,lqad->qlab", u_in, back, precision=HIGH)
    return back.astype(jnp.bfloat16)


def on_device(doc, close, pool_grads, doc_ids, query_grads, u_out, u_in, eigval):
    layers, share, queries = query_grads.shape
    mine = queries // doc
    parts = query_grads.transpose(2, 0, 1).reshape(doc, mine * layers, share)
    parts = lax.all_to_all(parts, "doc", 0, 0, tiled=True)
    raw = parts.reshape(doc, mine, layers, share).transpose(1, 2, 0, 3)
    raw = raw.reshape(mine, layers, D_OUT, D_IN).astype(jnp.float32)
    own = precondition(raw, u_out, u_in, eigval).reshape(mine, layers * D_OUT * D_IN)
    if close:
        whole = gather_chips(own, doc)
    else:
        whole = lax.all_gather(own, "doc", axis=0, tiled=True)
    total = None
    width = D_OUT * D_IN
    for layer in range(layers):
        term = lax.dot_general(
            whole[:, layer * width:(layer + 1) * width], pool_grads[layer],
            (((1,), (1,)), ((), ())), preferred_element_type=jnp.float32,
        )
        total = term if total is None else total + term
    stored = lax.broadcasted_iota(jnp.int32, (pool_grads.shape[1], doc_ids.shape[1]), 0)
    pick = (stored == doc_ids[0][None, :]).astype(jnp.float32)
    total = jnp.dot(total, pick, precision=HIGH)
    total = lax.psum_scatter(total, "layer", scatter_dimension=0, tiled=True)
    return total * (1.0 / math.sqrt(D_OUT * D_IN))


def solution(mesh):
    doc = mesh.shape["doc"]
    close = mesh.shape["win"] == 1 and mesh.shape["layer"] == 1 and doc % 8 == 0
    in_specs = (
        P("layer", ("win", "doc"), None),
        P(("win", "doc"), None),
        P("layer", "doc", None),
        P("layer", None, None),
        P("layer", None, None),
        P("layer", None, None),
    )
    out_specs = P("layer", ("win", "doc"))
    return jax.shard_map(
        functools.partial(on_device, doc, close),
        mesh=mesh, in_specs=in_specs, out_specs=out_specs, check_vma=False,
    )
```

```python
import functools
import math

import jax
import jax.numpy as jnp
from jax import lax
from jax.experimental import pallas as pl
from jax.experimental.pallas import tpu as pltpu
from jax.sharding import PartitionSpec as P

D_OUT = 64
D_IN = 64

HIGH = lax.Precision.HIGHEST
DAMPING = 0.05
MESH = pl.DeviceIdType.MESH


def gather_kernel(nz, own_ref, out, rz, rx, ry, rxh, ryh, rc, su, sd, sx, sy, sxh, syh, sc, local):
    me = lax.axis_index("doc")
    rows, cols = own_ref.shape
    half = cols // 2
    z = me // 8
    low = lax.rem(me, 8)
    core = lax.rem(low, 2)
    x = lax.rem(low // 2, 2)
    y = low // 4
    base = low - core
    col_x = base + 2 - 4 * x
    col_y = base + 4 - 8 * y
    col_xy = base + 6 - 4 * x - 8 * y
    z0 = z * 8
    to_x = z0 + col_x + core
    to_y = z0 + col_y + core
    to_c = z0 + base + 1 - core

    barrier = pltpu.get_barrier_semaphore()
    for who in (to_x, to_y, to_c):
        pl.semaphore_signal(barrier, inc=1, device_id={"doc": who}, device_id_type=MESH)

    @pl.when(z < nz - 1)
    def _():
        pl.semaphore_signal(barrier, inc=1, device_id={"doc": me + 8}, device_id_type=MESH)

    @pl.when(z > 0)
    def _():
        pl.semaphore_signal(barrier, inc=1, device_id={"doc": me - 8}, device_id_type=MESH)

    pl.semaphore_wait(barrier, 3 + jnp.minimum(z, 1) + jnp.minimum(nz - 1 - z, 1))

    def block(column, zs, c, part=None):
        row = pl.multiple_of((zs * 8 + column + c) * rows, rows)
        if part is None:
            return out.at[pl.ds(row, rows), :]
        return out.at[pl.ds(row, rows), pl.ds(part * half, half)]

    def copy(ref, dst, send, recv, who):
        return pltpu.make_async_remote_copy(
            src_ref=ref, dst_ref=dst, send_sem=send, recv_sem=recv,
            device_id={"doc": who}, device_id_type=MESH,
        )

    def up(zs, ref):
        return copy(ref, block(base, zs, core), su.at[zs], rz.at[zs], me + 8)

    def down(zs, ref):
        return copy(ref, block(base, zs, core), sd.at[zs], rz.at[zs], me - 8)

    def along_x(zs, ref):
        return copy(ref, block(base, zs, core), sx.at[zs], rx.at[zs], to_x)

    def along_y(zs, ref):
        return copy(ref, block(base, zs, core), sy.at[zs], ry.at[zs], to_y)

    def half_x(zs):
        b = block(col_y, zs, core, 1)
        return copy(b, b, sxh.at[zs], rxh.at[zs], to_x)

    def half_y(zs):
        b = block(col_x, zs, core, 0)
        return copy(b, b, syh.at[zs], ryh.at[zs], to_y)

    def other(kind, zs, ref, b):
        at = zs + kind * nz
        return copy(ref, b, sc.at[at], rc.at[at], to_c)

    own_block = block(base, z, core)
    keep = pltpu.make_async_copy(own_ref, own_block, local)

    def column_out(zs, ref):
        along_x(zs, ref).start()
        along_y(zs, ref).start()
        other(0, zs, ref, block(base, zs, core)).start()

    def steps(k, act):
        if k == 0:
            act(z, 0)
            return

        @pl.when(z - k >= 0)
        def _():
            act(z - k, 1)

        @pl.when(z + k < nz)
        def _():
            act(z + k, -1)

    def from_column(zs, way):
        b = block(base, zs, core)
        if way == 1:
            copy(b, b, su.at[zs], rz.at[zs], me - 8).wait_recv()

            @pl.when(z < nz - 1)
            def _():
                up(zs, b).start()
        else:
            copy(b, b, sd.at[zs], rz.at[zs], me + 8).wait_recv()

            @pl.when(z > 0)
            def _():
                down(zs, b).start()
        column_out(zs, b)

    def from_sides(zs, way):
        b = block(col_x, zs, core)
        copy(b, b, sx.at[zs], rx.at[zs], to_x).wait_recv()
        half_y(zs).start()
        other(1, zs, b, b).start()
        b = block(col_y, zs, core)
        copy(b, b, sy.at[zs], ry.at[zs], to_y).wait_recv()
        half_x(zs).start()
        other(2, zs, b, b).start()

    def from_corner(zs, way):
        b = block(col_xy, zs, core, 1)
        copy(b, b, sxh.at[zs], rxh.at[zs], to_x).wait_recv()
        other(3, zs, b, b).start()
        b = block(col_xy, zs, core, 0)
        copy(b, b, syh.at[zs], ryh.at[zs], to_y).wait_recv()
        other(4, zs, b, b).start()

    @pl.when(z < nz - 1)
    def _():
        up(z, own_ref).start()

    @pl.when(z > 0)
    def _():
        down(z, own_ref).start()

    column_out(z, own_ref)
    keep.start()
    for k in range(1, nz):
        steps(k, from_column)
        steps(k - 1, from_sides)
    steps(nz - 1, from_sides)
    for k in range(nz):
        steps(k, from_corner)

    keep.wait()
    for zs in range(nz):
        b = block(base, zs, core)
        along_x(zs, b).wait_send()
        along_y(zs, b).wait_send()
        half_x(zs).wait_send()
        half_y(zs).wait_send()

        @pl.when((z < nz - 1) & (zs <= z))
        def _():
            up(zs, b).wait_send()

        @pl.when((z > 0) & (zs >= z))
        def _():
            down(zs, b).wait_send()

        for kind, column, part in ((0, base, None), (1, col_x, None), (2, col_y, None), (3, col_xy, 1), (4, col_xy, 0)):
            b = block(column, zs, core, part)
            other(kind, zs, b, b).wait_send()
            b = block(column, zs, 1 - core, part)
            other(kind, zs, b, b).wait_recv()


def gather_chips(own, doc):
    nz = doc // 8
    rows, cols = own.shape
    dma = pltpu.SemaphoreType.DMA
    return pl.pallas_call(
        functools.partial(gather_kernel, nz),
        out_shape=jax.ShapeDtypeStruct((rows * doc, cols), own.dtype),
        in_specs=[pl.BlockSpec(memory_space=pl.ANY)],
        out_specs=pl.BlockSpec(memory_space=pl.ANY),
        scratch_shapes=[dma((nz,))] * 5 + [dma((5 * nz,))] + [dma((nz,))] * 6 + [dma((5 * nz,)), dma],
        compiler_params=pltpu.CompilerParams(collective_id=0, has_side_effects=True),
    )(own)


def exchange_kernel(doc, parts, out, send, recv, local):
    me = lax.axis_index("doc")
    barrier = pltpu.get_barrier_semaphore()

    @pl.loop(1, doc)
    def _(j):
        pl.semaphore_signal(barrier, inc=1, device_id={"doc": lax.rem(me + j, doc)}, device_id_type=MESH)

    pl.semaphore_wait(barrier, doc - 1)
    keep = pltpu.make_async_copy(parts.at[me], out.at[me], local)
    keep.start()

    def copy(j, to, at):
        return pltpu.make_async_remote_copy(
            src_ref=parts.at[to], dst_ref=out.at[at], send_sem=send.at[j], recv_sem=recv.at[j],
            device_id={"doc": to}, device_id_type=MESH,
        )

    @pl.loop(1, doc)
    def _(j):
        copy(j, lax.rem(me + j, doc), me).start()

    keep.wait()

    @pl.loop(1, doc)
    def _(j):
        copy(j, lax.rem(me + j, doc), lax.rem(me - j + doc, doc)).wait()


def exchange(parts, doc):
    dma = pltpu.SemaphoreType.DMA
    return pl.pallas_call(
        functools.partial(exchange_kernel, doc),
        out_shape=jax.ShapeDtypeStruct(parts.shape, parts.dtype),
        in_specs=[pl.BlockSpec(memory_space=pl.ANY)],
        out_specs=pl.BlockSpec(memory_space=pl.ANY),
        scratch_shapes=[dma((doc,)), dma((doc,)), dma],
        compiler_params=pltpu.CompilerParams(collective_id=1, has_side_effects=True),
    )(parts)


def score_kernel(ids, prepared, docs, out):
    at = pl.program_id(0)

    @pl.when(at == 0)
    def _():
        out[...] = jnp.zeros_like(out)

    out[...] += lax.dot_general(
        prepared[...], docs[0], (((1,), (1,)), ((), ())), preferred_element_type=jnp.float32
    )

    @pl.when(at == pl.num_programs(0) - 1)
    def _():
        stored = lax.broadcasted_iota(jnp.int32, (docs.shape[1], ids.shape[1]), 0)
        pick = jnp.where(stored == ids[...], 1.0, 0.0).astype(jnp.bfloat16)
        rest = out[...]
        total = None
        for _ in range(3):
            part = rest.astype(jnp.bfloat16)
            rest = rest - part.astype(jnp.float32)
            term = jnp.dot(part, pick, preferred_element_type=jnp.float32)
            total = term if total is None else total + term
        out[...] = total * (1.0 / math.sqrt(D_OUT * D_IN))


def score(ids, prepared, docs):
    layers, stored, width = docs.shape
    queries = prepared.shape[0]
    depth = 1024
    cuts = width // depth
    return pl.pallas_call(
        score_kernel,
        grid=(layers * cuts,),
        out_shape=jax.ShapeDtypeStruct((queries, ids.shape[1]), jnp.float32),
        in_specs=[
            pl.BlockSpec(ids.shape, lambda k: (0, 0)),
            pl.BlockSpec((queries, depth), lambda k: (0, k)),
            pl.BlockSpec((1, stored, depth), lambda k: (k // cuts, 0, k % cuts)),
        ],
        out_specs=pl.BlockSpec((queries, ids.shape[1]), lambda k: (0, 0)),
        compiler_params=pltpu.CompilerParams(
            dimension_semantics=("arbitrary",), vmem_limit_bytes=32 * 1024 * 1024
        ),
    )(ids, prepared, docs)


def precondition(raw, u_out, u_in, eigval):
    rotated = jnp.einsum("lac,qlab->lqcb", u_out, raw, precision=HIGH)
    rotated = jnp.einsum("lbd,lqcb->lqcd", u_in, rotated, precision=HIGH)
    scaled = rotated / (eigval[:, None] + DAMPING)
    back = jnp.einsum("lac,lqcd->lqad", u_out, scaled, precision=HIGH)
    back = jnp.einsum("lbd,lqad->qlab", u_in, back, precision=HIGH)
    return back.astype(jnp.bfloat16)


def on_device(doc, close, pool_grads, doc_ids, query_grads, u_out, u_in, eigval):
    layers, share, queries = query_grads.shape
    mine = queries // doc
    parts = query_grads.transpose(2, 0, 1).reshape(doc, mine * layers, share)
    if close:
        parts = exchange(parts, doc)
    else:
        parts = lax.all_to_all(parts, "doc", 0, 0, tiled=True)
    raw = parts.reshape(doc, mine, layers, share).transpose(1, 2, 0, 3)
    raw = raw.reshape(mine, layers, D_OUT, D_IN).astype(jnp.float32)
    own = precondition(raw, u_out, u_in, eigval).reshape(mine, layers * D_OUT * D_IN)
    if close:
        whole = gather_chips(own, doc)
    else:
        whole = lax.all_gather(own, "doc", axis=0, tiled=True)
    total = score(doc_ids, whole, pool_grads)
    return lax.psum_scatter(total, "layer", scatter_dimension=0, tiled=True)


def solution(mesh):
    doc = mesh.shape["doc"]
    close = mesh.shape["win"] == 1 and mesh.shape["layer"] == 1 and doc % 8 == 0
    in_specs = (
        P("layer", ("win", "doc"), None),
        P(("win", "doc"), None),
        P("layer", "doc", None),
        P("layer", None, None),
        P("layer", None, None),
        P("layer", None, None),
    )
    out_specs = P("layer", ("win", "doc"))
    return jax.shard_map(
        functools.partial(on_device, doc, close),
        mesh=mesh, in_specs=in_specs, out_specs=out_specs, check_vma=False,
    )
```

```python
import functools
import math

import jax
import jax.numpy as jnp
from jax import lax
from jax.experimental import pallas as pl
from jax.experimental.pallas import tpu as pltpu
from jax.sharding import PartitionSpec as P

D_OUT = 64
D_IN = 64

HIGH = lax.Precision.HIGHEST
DAMPING = 0.05
MESH = pl.DeviceIdType.MESH


def gather_kernel(nz, own_ref, out, rz, rx, ry, rxh, ryh, rc, su, sd, sx, sy, sxh, syh, sc, local):
    me = lax.axis_index("doc")
    rows, cols = own_ref.shape
    half = cols // 2
    z = me // 8
    low = lax.rem(me, 8)
    core = lax.rem(low, 2)
    x = lax.rem(low // 2, 2)
    y = low // 4
    base = low - core
    col_x = base + 2 - 4 * x
    col_y = base + 4 - 8 * y
    col_xy = base + 6 - 4 * x - 8 * y
    z0 = z * 8
    to_x = z0 + col_x + core
    to_y = z0 + col_y + core
    to_c = z0 + base + 1 - core

    barrier = pltpu.get_barrier_semaphore()
    for who in (to_x, to_y, to_c):
        pl.semaphore_signal(barrier, inc=1, device_id={"doc": who}, device_id_type=MESH)

    @pl.when(z < nz - 1)
    def _():
        pl.semaphore_signal(barrier, inc=1, device_id={"doc": me + 8}, device_id_type=MESH)

    @pl.when(z > 0)
    def _():
        pl.semaphore_signal(barrier, inc=1, device_id={"doc": me - 8}, device_id_type=MESH)

    pl.semaphore_wait(barrier, 3 + jnp.minimum(z, 1) + jnp.minimum(nz - 1 - z, 1))

    def block(column, zs, c, part=None):
        row = pl.multiple_of((zs * 8 + column + c) * rows, rows)
        if part is None:
            return out.at[pl.ds(row, rows), :]
        return out.at[pl.ds(row, rows), pl.ds(part * half, half)]

    def copy(ref, dst, send, recv, who):
        return pltpu.make_async_remote_copy(
            src_ref=ref, dst_ref=dst, send_sem=send, recv_sem=recv,
            device_id={"doc": who}, device_id_type=MESH,
        )

    def up(zs, ref):
        return copy(ref, block(base, zs, core), su.at[zs], rz.at[zs], me + 8)

    def down(zs, ref):
        return copy(ref, block(base, zs, core), sd.at[zs], rz.at[zs], me - 8)

    def along_x(zs, ref):
        return copy(ref, block(base, zs, core), sx.at[zs], rx.at[zs], to_x)

    def along_y(zs, ref):
        return copy(ref, block(base, zs, core), sy.at[zs], ry.at[zs], to_y)

    def half_x(zs):
        b = block(col_y, zs, core, 1)
        return copy(b, b, sxh.at[zs], rxh.at[zs], to_x)

    def half_y(zs):
        b = block(col_x, zs, core, 0)
        return copy(b, b, syh.at[zs], ryh.at[zs], to_y)

    def other(kind, zs, ref, b):
        at = zs + kind * nz
        return copy(ref, b, sc.at[at], rc.at[at], to_c)

    own_block = block(base, z, core)
    keep = pltpu.make_async_copy(own_ref, own_block, local)

    def column_out(zs, ref):
        along_x(zs, ref).start()
        along_y(zs, ref).start()
        other(0, zs, ref, block(base, zs, core)).start()

    def steps(k, act):
        if k == 0:
            act(z, 0)
            return

        @pl.when(z - k >= 0)
        def _():
            act(z - k, 1)

        @pl.when(z + k < nz)
        def _():
            act(z + k, -1)

    def from_column(zs, way):
        b = block(base, zs, core)
        if way == 1:
            copy(b, b, su.at[zs], rz.at[zs], me - 8).wait_recv()

            @pl.when(z < nz - 1)
            def _():
                up(zs, b).start()
        else:
            copy(b, b, sd.at[zs], rz.at[zs], me + 8).wait_recv()

            @pl.when(z > 0)
            def _():
                down(zs, b).start()
        column_out(zs, b)

    def from_sides(zs, way):
        b = block(col_x, zs, core)
        copy(b, b, sx.at[zs], rx.at[zs], to_x).wait_recv()
        half_y(zs).start()
        other(1, zs, b, b).start()
        b = block(col_y, zs, core)
        copy(b, b, sy.at[zs], ry.at[zs], to_y).wait_recv()
        half_x(zs).start()
        other(2, zs, b, b).start()

    def from_corner(zs, way):
        b = block(col_xy, zs, core, 1)
        copy(b, b, sxh.at[zs], rxh.at[zs], to_x).wait_recv()
        other(3, zs, b, b).start()
        b = block(col_xy, zs, core, 0)
        copy(b, b, syh.at[zs], ryh.at[zs], to_y).wait_recv()
        other(4, zs, b, b).start()

    @pl.when(z < nz - 1)
    def _():
        up(z, own_ref).start()

    @pl.when(z > 0)
    def _():
        down(z, own_ref).start()

    column_out(z, own_ref)
    keep.start()
    for k in range(1, nz):
        steps(k, from_column)
        steps(k - 1, from_sides)
    steps(nz - 1, from_sides)
    for k in range(nz):
        steps(k, from_corner)

    keep.wait()
    for zs in range(nz):
        b = block(base, zs, core)
        along_x(zs, b).wait_send()
        along_y(zs, b).wait_send()
        half_x(zs).wait_send()
        half_y(zs).wait_send()

        @pl.when((z < nz - 1) & (zs <= z))
        def _():
            up(zs, b).wait_send()

        @pl.when((z > 0) & (zs >= z))
        def _():
            down(zs, b).wait_send()

        for kind, column, part in ((0, base, None), (1, col_x, None), (2, col_y, None), (3, col_xy, 1), (4, col_xy, 0)):
            b = block(column, zs, core, part)
            other(kind, zs, b, b).wait_send()
            b = block(column, zs, 1 - core, part)
            other(kind, zs, b, b).wait_recv()


def gather_chips(own, doc):
    nz = doc // 8
    rows, cols = own.shape
    dma = pltpu.SemaphoreType.DMA
    return pl.pallas_call(
        functools.partial(gather_kernel, nz),
        out_shape=jax.ShapeDtypeStruct((rows * doc, cols), own.dtype),
        in_specs=[pl.BlockSpec(memory_space=pl.ANY)],
        out_specs=pl.BlockSpec(memory_space=pl.ANY),
        scratch_shapes=[dma((nz,))] * 5 + [dma((5 * nz,))] + [dma((nz,))] * 6 + [dma((5 * nz,)), dma],
        compiler_params=pltpu.CompilerParams(collective_id=0, has_side_effects=True),
    )(own)


def exchange_kernel(doc, parts, out, send, recv, local):
    me = lax.axis_index("doc")
    barrier = pltpu.get_barrier_semaphore()

    @pl.loop(1, doc)
    def _(j):
        pl.semaphore_signal(barrier, inc=1, device_id={"doc": lax.rem(me + j, doc)}, device_id_type=MESH)

    pl.semaphore_wait(barrier, doc - 1)
    keep = pltpu.make_async_copy(parts.at[me], out.at[me], local)
    keep.start()

    def copy(j, to, at):
        return pltpu.make_async_remote_copy(
            src_ref=parts.at[to], dst_ref=out.at[at], send_sem=send.at[j], recv_sem=recv.at[j],
            device_id={"doc": to}, device_id_type=MESH,
        )

    @pl.loop(1, doc)
    def _(j):
        copy(j, lax.rem(me + j, doc), me).start()

    keep.wait()

    @pl.loop(1, doc)
    def _(j):
        copy(j, lax.rem(me + j, doc), lax.rem(me - j + doc, doc)).wait()


def exchange(parts, doc):
    dma = pltpu.SemaphoreType.DMA
    return pl.pallas_call(
        functools.partial(exchange_kernel, doc),
        out_shape=jax.ShapeDtypeStruct(parts.shape, parts.dtype),
        in_specs=[pl.BlockSpec(memory_space=pl.ANY)],
        out_specs=pl.BlockSpec(memory_space=pl.ANY),
        scratch_shapes=[dma((doc,)), dma((doc,)), dma],
        compiler_params=pltpu.CompilerParams(collective_id=1, has_side_effects=True),
    )(parts)


def score_kernel(ids, prepared, docs, out):
    at = pl.program_id(0)

    @pl.when(at == 0)
    def _():
        out[...] = jnp.zeros_like(out)

    out[...] += lax.dot_general(
        prepared[...], docs[0], (((1,), (1,)), ((), ())), preferred_element_type=jnp.float32
    )

    @pl.when(at == pl.num_programs(0) - 1)
    def _():
        stored = lax.broadcasted_iota(jnp.int32, (docs.shape[1], ids.shape[1]), 0)
        pick = jnp.where(stored == ids[...], 1.0, 0.0).astype(jnp.bfloat16)
        rest = out[...]
        total = None
        for _ in range(3):
            part = rest.astype(jnp.bfloat16)
            rest = rest - part.astype(jnp.float32)
            term = jnp.dot(part, pick, preferred_element_type=jnp.float32)
            total = term if total is None else total + term
        out[...] = total * (1.0 / math.sqrt(D_OUT * D_IN))


def score(ids, prepared, docs):
    layers, stored, width = docs.shape
    queries = prepared.shape[0]
    depth = 2048
    cuts = width // depth
    return pl.pallas_call(
        score_kernel,
        grid=(layers * cuts,),
        out_shape=jax.ShapeDtypeStruct((queries, ids.shape[1]), jnp.float32),
        in_specs=[
            pl.BlockSpec(ids.shape, lambda k: (0, 0)),
            pl.BlockSpec((queries, depth), lambda k: (0, k)),
            pl.BlockSpec((1, stored, depth), lambda k: (k // cuts, 0, k % cuts)),
        ],
        out_specs=pl.BlockSpec((queries, ids.shape[1]), lambda k: (0, 0)),
        compiler_params=pltpu.CompilerParams(
            dimension_semantics=("arbitrary",), vmem_limit_bytes=60 * 1024 * 1024
        ),
    )(ids, prepared, docs)


def precondition(raw, u_out, u_in, eigval):
    rotated = jnp.einsum("lac,qlab->lqcb", u_out, raw, precision=HIGH)
    rotated = jnp.einsum("lbd,lqcb->lqcd", u_in, rotated, precision=HIGH)
    scaled = rotated / (eigval[:, None] + DAMPING)
    back = jnp.einsum("lac,lqcd->lqad", u_out, scaled, precision=HIGH)
    back = jnp.einsum("lbd,lqad->qlab", u_in, back, precision=HIGH)
    return back.astype(jnp.bfloat16)


def on_device(doc, close, pool_grads, doc_ids, query_grads, u_out, u_in, eigval):
    layers, share, queries = query_grads.shape
    mine = queries // doc
    parts = query_grads.transpose(2, 0, 1).reshape(doc, mine * layers, share)
    if close:
        parts = exchange(parts, doc)
    else:
        parts = lax.all_to_all(parts, "doc", 0, 0, tiled=True)
    raw = parts.reshape(doc, mine, layers, share).transpose(1, 2, 0, 3)
    raw = raw.reshape(mine, layers, D_OUT, D_IN).astype(jnp.float32)
    own = precondition(raw, u_out, u_in, eigval).reshape(mine, layers * D_OUT * D_IN)
    if close:
        whole = gather_chips(own, doc)
    else:
        whole = lax.all_gather(own, "doc", axis=0, tiled=True)
    total = score(doc_ids, whole, pool_grads)
    return lax.psum_scatter(total, "layer", scatter_dimension=0, tiled=True)


def solution(mesh):
    doc = mesh.shape["doc"]
    close = mesh.shape["win"] == 1 and mesh.shape["layer"] == 1 and doc % 8 == 0
    in_specs = (
        P("layer", ("win", "doc"), None),
        P(("win", "doc"), None),
        P("layer", "doc", None),
        P("layer", None, None),
        P("layer", None, None),
        P("layer", None, None),
    )
    out_specs = P("layer", ("win", "doc"))
    return jax.shard_map(
        functools.partial(on_device, doc, close),
        mesh=mesh, in_specs=in_specs, out_specs=out_specs, check_vma=False,
    )
```

```python
import functools
import math

import jax
import jax.numpy as jnp
from jax import lax
from jax.experimental import pallas as pl
from jax.experimental.pallas import tpu as pltpu
from jax.sharding import PartitionSpec as P

D_OUT = 64
D_IN = 64

HIGH = lax.Precision.HIGH
DAMPING = 0.05
MESH = pl.DeviceIdType.MESH


def gather_kernel(nz, own_ref, out, rz, rx, ry, rxh, ryh, rc, su, sd, sx, sy, sxh, syh, sc, local):
    me = lax.axis_index("doc")
    rows, cols = own_ref.shape
    half = cols // 2
    z = me // 8
    low = lax.rem(me, 8)
    core = lax.rem(low, 2)
    x = lax.rem(low // 2, 2)
    y = low // 4
    base = low - core
    col_x = base + 2 - 4 * x
    col_y = base + 4 - 8 * y
    col_xy = base + 6 - 4 * x - 8 * y
    z0 = z * 8
    to_x = z0 + col_x + core
    to_y = z0 + col_y + core
    to_c = z0 + base + 1 - core

    barrier = pltpu.get_barrier_semaphore()
    for who in (to_x, to_y, to_c):
        pl.semaphore_signal(barrier, inc=1, device_id={"doc": who}, device_id_type=MESH)

    @pl.when(z < nz - 1)
    def _():
        pl.semaphore_signal(barrier, inc=1, device_id={"doc": me + 8}, device_id_type=MESH)

    @pl.when(z > 0)
    def _():
        pl.semaphore_signal(barrier, inc=1, device_id={"doc": me - 8}, device_id_type=MESH)

    pl.semaphore_wait(barrier, 3 + jnp.minimum(z, 1) + jnp.minimum(nz - 1 - z, 1))

    def block(column, zs, c, part=None):
        row = pl.multiple_of((zs * 8 + column + c) * rows, rows)
        if part is None:
            return out.at[pl.ds(row, rows), :]
        return out.at[pl.ds(row, rows), pl.ds(part * half, half)]

    def copy(ref, dst, send, recv, who):
        return pltpu.make_async_remote_copy(
            src_ref=ref, dst_ref=dst, send_sem=send, recv_sem=recv,
            device_id={"doc": who}, device_id_type=MESH,
        )

    def up(zs, ref):
        return copy(ref, block(base, zs, core), su.at[zs], rz.at[zs], me + 8)

    def down(zs, ref):
        return copy(ref, block(base, zs, core), sd.at[zs], rz.at[zs], me - 8)

    def along_x(zs, ref):
        return copy(ref, block(base, zs, core), sx.at[zs], rx.at[zs], to_x)

    def along_y(zs, ref):
        return copy(ref, block(base, zs, core), sy.at[zs], ry.at[zs], to_y)

    def half_x(zs):
        b = block(col_y, zs, core, 1)
        return copy(b, b, sxh.at[zs], rxh.at[zs], to_x)

    def half_y(zs):
        b = block(col_x, zs, core, 0)
        return copy(b, b, syh.at[zs], ryh.at[zs], to_y)

    def other(kind, zs, ref, b):
        at = zs + kind * nz
        return copy(ref, b, sc.at[at], rc.at[at], to_c)

    own_block = block(base, z, core)
    keep = pltpu.make_async_copy(own_ref, own_block, local)

    def column_out(zs, ref):
        along_x(zs, ref).start()
        along_y(zs, ref).start()
        other(0, zs, ref, block(base, zs, core)).start()

    def steps(k, act):
        if k == 0:
            act(z, 0)
            return

        @pl.when(z - k >= 0)
        def _():
            act(z - k, 1)

        @pl.when(z + k < nz)
        def _():
            act(z + k, -1)

    def from_column(zs, way):
        b = block(base, zs, core)
        if way == 1:
            copy(b, b, su.at[zs], rz.at[zs], me - 8).wait_recv()

            @pl.when(z < nz - 1)
            def _():
                up(zs, b).start()
        else:
            copy(b, b, sd.at[zs], rz.at[zs], me + 8).wait_recv()

            @pl.when(z > 0)
            def _():
                down(zs, b).start()
        column_out(zs, b)

    def from_sides(zs, way):
        b = block(col_x, zs, core)
        copy(b, b, sx.at[zs], rx.at[zs], to_x).wait_recv()
        half_y(zs).start()
        other(1, zs, b, b).start()
        b = block(col_y, zs, core)
        copy(b, b, sy.at[zs], ry.at[zs], to_y).wait_recv()
        half_x(zs).start()
        other(2, zs, b, b).start()

    def from_corner(zs, way):
        b = block(col_xy, zs, core, 1)
        copy(b, b, sxh.at[zs], rxh.at[zs], to_x).wait_recv()
        other(3, zs, b, b).start()
        b = block(col_xy, zs, core, 0)
        copy(b, b, syh.at[zs], ryh.at[zs], to_y).wait_recv()
        other(4, zs, b, b).start()

    @pl.when(z < nz - 1)
    def _():
        up(z, own_ref).start()

    @pl.when(z > 0)
    def _():
        down(z, own_ref).start()

    column_out(z, own_ref)
    keep.start()
    for k in range(1, nz):
        steps(k, from_column)
        steps(k - 1, from_sides)
    steps(nz - 1, from_sides)
    for k in range(nz):
        steps(k, from_corner)

    keep.wait()
    for zs in range(nz):
        b = block(base, zs, core)
        along_x(zs, b).wait_send()
        along_y(zs, b).wait_send()
        half_x(zs).wait_send()
        half_y(zs).wait_send()

        @pl.when((z < nz - 1) & (zs <= z))
        def _():
            up(zs, b).wait_send()

        @pl.when((z > 0) & (zs >= z))
        def _():
            down(zs, b).wait_send()

        for kind, column, part in ((0, base, None), (1, col_x, None), (2, col_y, None), (3, col_xy, 1), (4, col_xy, 0)):
            b = block(column, zs, core, part)
            other(kind, zs, b, b).wait_send()
            b = block(column, zs, 1 - core, part)
            other(kind, zs, b, b).wait_recv()


def gather_chips(own, doc):
    nz = doc // 8
    rows, cols = own.shape
    dma = pltpu.SemaphoreType.DMA
    return pl.pallas_call(
        functools.partial(gather_kernel, nz),
        out_shape=jax.ShapeDtypeStruct((rows * doc, cols), own.dtype),
        in_specs=[pl.BlockSpec(memory_space=pl.ANY)],
        out_specs=pl.BlockSpec(memory_space=pl.ANY),
        scratch_shapes=[dma((nz,))] * 5 + [dma((5 * nz,))] + [dma((nz,))] * 6 + [dma((5 * nz,)), dma],
        compiler_params=pltpu.CompilerParams(collective_id=0, has_side_effects=True),
    )(own)


def exchange_kernel(doc, parts, out, send, recv, local):
    me = lax.axis_index("doc")
    barrier = pltpu.get_barrier_semaphore()

    @pl.loop(1, doc)
    def _(j):
        pl.semaphore_signal(barrier, inc=1, device_id={"doc": lax.rem(me + j, doc)}, device_id_type=MESH)

    pl.semaphore_wait(barrier, doc - 1)
    keep = pltpu.make_async_copy(parts.at[me], out.at[me], local)
    keep.start()

    def copy(j, to, at):
        return pltpu.make_async_remote_copy(
            src_ref=parts.at[to], dst_ref=out.at[at], send_sem=send.at[j], recv_sem=recv.at[j],
            device_id={"doc": to}, device_id_type=MESH,
        )

    @pl.loop(1, doc)
    def _(j):
        copy(j, lax.rem(me + j, doc), me).start()

    keep.wait()

    @pl.loop(1, doc)
    def _(j):
        copy(j, lax.rem(me + j, doc), lax.rem(me - j + doc, doc)).wait()


def exchange(parts, doc):
    dma = pltpu.SemaphoreType.DMA
    return pl.pallas_call(
        functools.partial(exchange_kernel, doc),
        out_shape=jax.ShapeDtypeStruct(parts.shape, parts.dtype),
        in_specs=[pl.BlockSpec(memory_space=pl.ANY)],
        out_specs=pl.BlockSpec(memory_space=pl.ANY),
        scratch_shapes=[dma((doc,)), dma((doc,)), dma],
        compiler_params=pltpu.CompilerParams(collective_id=1, has_side_effects=True),
    )(parts)


def score_kernel(ids, prepared, docs, out):
    at = pl.program_id(0)

    @pl.when(at == 0)
    def _():
        out[...] = jnp.zeros_like(out)

    out[...] += lax.dot_general(
        prepared[...], docs[0], (((1,), (1,)), ((), ())), preferred_element_type=jnp.float32
    )

    @pl.when(at == pl.num_programs(0) - 1)
    def _():
        stored = lax.broadcasted_iota(jnp.int32, (docs.shape[1], ids.shape[1]), 0)
        pick = jnp.where(stored == ids[...], 1.0, 0.0).astype(jnp.bfloat16)
        rest = out[...]
        total = None
        for _ in range(3):
            part = rest.astype(jnp.bfloat16)
            rest = rest - part.astype(jnp.float32)
            term = jnp.dot(part, pick, preferred_element_type=jnp.float32)
            total = term if total is None else total + term
        out[...] = total * (1.0 / math.sqrt(D_OUT * D_IN))


def score(ids, prepared, docs):
    layers, stored, width = docs.shape
    queries = prepared.shape[0]
    depth = 1024
    cuts = width // depth
    return pl.pallas_call(
        score_kernel,
        grid=(layers * cuts,),
        out_shape=jax.ShapeDtypeStruct((queries, ids.shape[1]), jnp.float32),
        in_specs=[
            pl.BlockSpec(ids.shape, lambda k: (0, 0)),
            pl.BlockSpec((queries, depth), lambda k: (0, k)),
            pl.BlockSpec((1, stored, depth), lambda k: (k // cuts, 0, k % cuts)),
        ],
        out_specs=pl.BlockSpec((queries, ids.shape[1]), lambda k: (0, 0)),
        compiler_params=pltpu.CompilerParams(
            dimension_semantics=("arbitrary",), vmem_limit_bytes=60 * 1024 * 1024
        ),
    )(ids, prepared, docs)


def precondition(raw, u_out, u_in, eigval):
    rotated = jnp.einsum("lac,qlab->lqcb", u_out, raw, precision=HIGH)
    rotated = jnp.einsum("lbd,lqcb->lqcd", u_in, rotated, precision=HIGH)
    scaled = rotated * (1.0 / (eigval + DAMPING))[:, None]
    back = jnp.einsum("lac,lqcd->lqad", u_out, scaled, precision=HIGH)
    back = jnp.einsum("lbd,lqad->qlab", u_in, back, precision=HIGH)
    return back.astype(jnp.bfloat16)


def on_device(doc, close, pool_grads, doc_ids, query_grads, u_out, u_in, eigval):
    layers, share, queries = query_grads.shape
    mine = queries // doc
    parts = query_grads.transpose(2, 0, 1).reshape(doc, mine * layers, share)
    if close:
        parts = exchange(parts, doc)
    else:
        parts = lax.all_to_all(parts, "doc", 0, 0, tiled=True)
    raw = parts.reshape(doc, mine, layers, share).transpose(1, 2, 0, 3)
    raw = raw.reshape(mine, layers, D_OUT, D_IN).astype(jnp.float32)
    own = precondition(raw, u_out, u_in, eigval).reshape(mine, layers * D_OUT * D_IN)
    if close:
        whole = gather_chips(own, doc)
    else:
        whole = lax.all_gather(own, "doc", axis=0, tiled=True)
    total = score(doc_ids, whole, pool_grads)
    return lax.psum_scatter(total, "layer", scatter_dimension=0, tiled=True)


def solution(mesh):
    doc = mesh.shape["doc"]
    close = mesh.shape["win"] == 1 and mesh.shape["layer"] == 1 and doc % 8 == 0
    in_specs = (
        P("layer", ("win", "doc"), None),
        P(("win", "doc"), None),
        P("layer", "doc", None),
        P("layer", None, None),
        P("layer", None, None),
        P("layer", None, None),
    )
    out_specs = P("layer", ("win", "doc"))
    return jax.shard_map(
        functools.partial(on_device, doc, close),
        mesh=mesh, in_specs=in_specs, out_specs=out_specs, check_vma=False,
    )
```
